32 devices in a mesh: dp: 8 (over y, x, core), seq: 4 (over z).
Axes of the slice: x: 2, y: 2, z: 4, core: 2. Of those that a mesh axis runs over, the one named last changes fastest.
Arguments:
- projections: bfloat16 [8, 4096, 3, 2048], P('dp', 'seq'), may hold values from -12 to 12
- doc_lengths: int32 [8, 8], P('dp'), may hold values from 1 to 2048, 4096 in all within a row
- latents: bfloat16 [64, 256, 128], P('dp'), may hold values from -6 to 6
- mix_weight: bfloat16 [128, 512], replicated, may hold values from -0.5 to 0.5
- head_weight: bfloat16 [512, 3, 2048], P(None, None, 'seq'), may hold values from -0.25 to 0.25
- image_row: int32 [64], replicated, may hold values from 0 to 7, as said below
- image_slot: int32 [64], replicated, may hold values from 0 to 15, as said below
Outputs:
- attended: bfloat16 [8, 4096, 2048], P('dp', 'seq')
The draws below stay inside these ranges and needn't reach their ends.
Inputs may be any that keep to these rules, and one draw needn't show every extreme that they name: `image_row`: each index of dp holds images 8 * o to 8 * o + 7; at most 2 of one index's images go to the same row, and that many do in every draw. `image_slot`: slot s of a row covers positions s * 256 to s * 256 + 255; the images of one row lie in distinct slots.
All inputs are finite; a program needn't handle non-finite values.
Results may differ from the reference program's by a relative error of at most 0.0078.
Values may be sent and summed in bfloat16 or wider, within the bound.
A program may use at most 256 MiB of HBM per device.

```python
import math
import jax
import jax.numpy as jnp
import numpy as np
from jax import lax

H = 16
E = 128
HID = 512
PIN = 128
P_SIZE = 256
DOCS = 8
LEN = 4096
IMG_DEV = 8
ROWS = 8
HD = 2048
SLOTS = 16
IMAGES = 64
N_DP = 8


def place_images(key):
    groups = N_DP
    key_rows, key_slots = jax.random.split(key)
    rank_ids = jnp.arange(groups, dtype=jnp.int32)
    spread = jnp.abs(2 * rank_ids - groups + 1)
    offset = IMG_DEV * spread // groups
    degree = jnp.where(2 * rank_ids > groups - 1, IMG_DEV + offset, IMG_DEV - offset).astype(jnp.int32)
    stub_ends = jnp.cumsum(degree).astype(jnp.int32)
    stub_starts = stub_ends - degree
    row_order = jax.random.permutation(key_rows, groups).astype(jnp.int32)
    image_ids = jnp.arange(IMAGES, dtype=jnp.int32)
    owner = image_ids // IMG_DEV
    local_index = image_ids % IMG_DEV
    stub_index = local_index * groups + owner
    row_rank = jnp.sum((stub_index[:, None] >= stub_ends[None, :]).astype(jnp.int32), axis=1).astype(jnp.int32)
    within_row = stub_index - stub_starts[row_rank]
    dest_row = row_order[row_rank]
    slot_keys = jax.random.split(key_slots, groups)
    slot_orders = jax.vmap(lambda single: jax.random.permutation(single, SLOTS))(slot_keys).astype(jnp.int32)
    dest_slot = slot_orders[dest_row, within_row]
    return (dest_row.astype(jnp.int32), dest_slot.astype(jnp.int32))


def draw_image_row(key, part):
    return place_images(key)[0]


def draw_image_slot(key, part):
    return place_images(key)[1]


def draw_projections(key, part):
    key = jax.random.fold_in(key, 7)
    full_shape = (ROWS, LEN, 3, HD)
    entries = jnp.clip(jax.random.normal(key, full_shape, jnp.float32), -6.0, 6.0)
    return entries.astype(jnp.bfloat16)


def shard_levels(own_key, dims, shards, smallest, high):
    gain, own = 1.0, jax.random.fold_in(own_key, 6)
    for dim, parts in shards:
        draws = jnp.exp(jax.random.uniform(jax.random.fold_in(own, dim), (parts,), jnp.float32, smallest / len(shards), high / len(shards)))
        gain = gain * jnp.repeat(draws, dims[dim] // parts).reshape([-1 if axis == dim else 1 for axis in range(len(dims))])
    return gain


def length_profile(amount, total, limit, slope):
    loads = [(1 << 20) // math.isqrt(grade ** slope) + 1 for grade in range(2, amount + 1)]
    spare, counts = total - limit - (amount - 1), [1] * (amount - 1)
    while spare > 0:
        movable = [i for i in range(amount - 1) if counts[i] < limit]
        whole, remaining = sum([loads[i] for i in movable]), spare
        for i in movable:
            extra = min(limit - counts[i], max(1, remaining * loads[i] // whole), spare)
            counts[i] = counts[i] + extra
            spare = spare - extra
    return np.array([limit] + counts)


def ragged(stream_key, number_of, total, limit, lean):
    if number_of == 2:
        one = jax.random.randint(stream_key, (), max(1, total - limit), min(limit, total - 1) + 1)
        return jnp.stack([one, total - one])
    sizes = jnp.asarray(length_profile(number_of, total, limit, lean), jnp.int32)
    couples = (number_of - 1) // 2
    giver, receiver = sizes[1:1 + 2 * couples:2], sizes[2:2 + 2 * couples:2]
    room = jnp.minimum(giver - 1, limit - receiver)
    shifted = jax.random.randint(jax.random.fold_in(stream_key, 1), (couples,), 0, 1 << 20) % (room + 1)
    sizes = sizes.at[1:1 + 2 * couples:2].set(giver - shifted).at[2:2 + 2 * couples:2].set(receiver + shifted)
    return sizes[jax.random.permutation(jax.random.fold_in(stream_key, 2), number_of)]


def centred(key, shape, scale, limit, cuts=(), kind=jnp.bfloat16):
    values = scale * jax.random.normal(key, shape, jnp.float32)
    if cuts:
        values = values * shard_levels(key, shape, cuts, -0.22, 0.18)
    return jnp.clip(values, -limit, limit).astype(kind)


def setup_inputs(seed: int = 0) -> dict:
    splits = jax.random.split(jax.random.key(seed), 8)
    projections = draw_projections(jax.random.fold_in(splits[7], 71), 0)
    doc_lengths = jax.vmap(lambda own: ragged(own, DOCS, LEN, LEN // 2, 2))(jax.random.split(splits[1], ROWS)).reshape((ROWS, DOCS)).astype(jnp.int32)
    latents = centred(splits[2], (IMAGES, P_SIZE, PIN), 1.0, 6.0, ((0, 8),))
    mix_weight = centred(splits[3], (PIN, HID), PIN ** -0.5, 0.5)
    head_weight = centred(splits[4], (HID, 3, HD), HID ** -0.5, 0.25, ((2, 4),))
    image_row = draw_image_row(jax.random.fold_in(splits[7], 71), 0)
    image_slot = draw_image_slot(jax.random.fold_in(splits[7], 71), 0)
    return dict(projections=projections, doc_lengths=doc_lengths, latents=latents, mix_weight=mix_weight, head_weight=head_weight, image_row=image_row, image_slot=image_slot)


EPSILON = 1e-05
MASKED = -1e+30

def down_block(patches, mix_weight):
    image_count, patch_count, patch_width = patches.shape
    mixed_rows = jnp.dot(patches.reshape(image_count * patch_count, patch_width), mix_weight, preferred_element_type=jnp.float32)
    scaled = mixed_rows * lax.rsqrt(lax.optimization_barrier(jnp.mean(mixed_rows * mixed_rows, axis=-1, keepdims=True)) + EPSILON)
    return jax.nn.silu(scaled).astype(jnp.bfloat16)

def project(hidden, head_weight):
    return jnp.dot(hidden, head_weight.reshape(head_weight.shape[0], -1), preferred_element_type=jnp.float32).astype(jnp.bfloat16)

def reference(projections, doc_lengths, latents, mix_weight, head_weight, image_row, image_slot):
    slot_count = LEN // P_SIZE
    flat_latents = latents.reshape(IMAGES, P_SIZE * PIN).astype(jnp.float32)
    block_size = min(512, LEN)
    scale = 1.0 / math.sqrt(E)

    def one_row(row_args):
        row_index, base, lengths = row_args
        slot_ids = jnp.arange(slot_count, dtype=jnp.int32)
        slot_picks = ((image_slot[None, :] == slot_ids[:, None]) & (image_row[None, :] == row_index)).astype(jnp.float32)
        gathered = jnp.dot(slot_picks, flat_latents, precision=lax.Precision.HIGHEST).astype(jnp.bfloat16).reshape(slot_count, P_SIZE, PIN)
        image_term = project(down_block(gathered, mix_weight), head_weight).reshape(LEN, 3, HD)
        combined = (base.astype(jnp.float32) + image_term.astype(jnp.float32)).astype(jnp.bfloat16)
        starts = (jnp.cumsum(lengths) - lengths).astype(jnp.int32)
        positions = jnp.arange(LEN, dtype=jnp.int32)
        doc_index = (lax.optimization_barrier(jnp.sum((positions[:, None] >= starts[None, :]).astype(jnp.int32), axis=1)) - 1).astype(jnp.int32)
        slot_used = lax.optimization_barrier(jnp.sum(slot_picks, axis=1)) > 0
        image_index = jnp.where(jnp.repeat(slot_used, P_SIZE), jnp.repeat(slot_ids, P_SIZE), -1).astype(jnp.int32)
        queries = combined[:, 0].reshape(LEN, H, E).astype(jnp.float32)
        keys = combined[:, 1].reshape(LEN, H, E).astype(jnp.float32)
        values = combined[:, 2].reshape(LEN, H, E).astype(jnp.float32)
        pieces = []
        for block_index in range(LEN // block_size):
            first_row = block_index * block_size
            key_end = first_row + block_size
            scores = jnp.einsum('qhe,khe->hqk', queries[first_row:key_end], keys[:key_end]) * scale
            doc_query = doc_index[first_row:key_end]
            image_query = image_index[first_row:key_end]
            allowed = (doc_query[:, None] == doc_index[None, :key_end]) & ((positions[None, :key_end] <= positions[first_row:key_end, None]) | (image_query[:, None] >= 0) & (image_query[:, None] == image_index[None, :key_end]))
            scores = jnp.where(allowed[None], scores, MASKED)
            largest = lax.optimization_barrier(jnp.max(scores, axis=-1, keepdims=True))
            weights = jnp.where(allowed[None], jnp.exp(scores - largest), 0.0)
            total = lax.optimization_barrier(jnp.sum(weights, axis=-1))
            rounded = weights.astype(jnp.bfloat16).astype(jnp.float32)
            result = jnp.einsum('hqk,khe->qhe', rounded, values[:key_end]) / jnp.transpose(total)[:, :, None]
            pieces.append(result.astype(jnp.bfloat16))
        return jnp.concatenate(pieces, axis=0).reshape(LEN, HD)
    return lax.map(one_row, (jnp.arange(ROWS, dtype=jnp.int32), projections, doc_lengths))
```

```python
import functools
import math

import jax
import jax.numpy as jnp
from jax import lax
from jax.experimental import pallas as pl
from jax.experimental.pallas import tpu as pltpu
from jax.sharding import PartitionSpec as P

E = 128
EPSILON = 1e-05
MASKED = -1e30
LOWEST = -1e29
LOG2E = 1.4426950408889634


def down_block(patches, mix_weight):
    mixed_rows = jnp.dot(patches, mix_weight, preferred_element_type=jnp.float32)
    scaled = mixed_rows * lax.rsqrt(
        jnp.mean(mixed_rows * mixed_rows, axis=-1, keepdims=True) + EPSILON
    )
    return jax.nn.silu(scaled).astype(jnp.bfloat16)


def flash_kernel(first_ref, last_ref, lo_ref, hi_ref, q_ref, k_ref, v_ref, o_ref, lse_ref,
                 m_ref, l_ref, acc_ref, *, heads, bk):
    i = pl.program_id(0)
    bq = q_ref.shape[0]
    lo = lo_ref[...]
    hi = hi_ref[...]
    scale = LOG2E / math.sqrt(E)
    m_ref[...] = jnp.full(m_ref.shape, LOWEST, jnp.float32)
    l_ref[...] = jnp.zeros(l_ref.shape, jnp.float32)
    acc_ref[...] = jnp.zeros(acc_ref.shape, jnp.float32)

    def step(j, carry):
        rows = pl.ds(pl.multiple_of(j * bk, bk), bk)
        u = j * bk + lax.broadcasted_iota(jnp.int32, (1, bk), 1)
        seen = (u >= lo) & (u <= hi)
        for h in range(heads):
            cols = slice(h * E, (h + 1) * E)
            s = lax.dot_general(
                q_ref[:, cols], k_ref[rows, cols], (((1,), (1,)), ((), ())),
                preferred_element_type=jnp.float32,
            ) * scale
            s = jnp.where(seen, s, MASKED)
            m_old = m_ref[h, :, :1]
            m_new = jnp.maximum(m_old, jnp.max(s, axis=1, keepdims=True))
            p = jnp.exp2(s - m_new)
            alpha = jnp.exp2(m_old - m_new)
            l_new = l_ref[h, :, :1] * alpha + jnp.sum(p, axis=1, keepdims=True)
            m_ref[h] = jnp.broadcast_to(m_new, (bq, E))
            l_ref[h] = jnp.broadcast_to(l_new, (bq, E))
            acc_ref[h] = acc_ref[h] * alpha + jnp.dot(
                p.astype(jnp.bfloat16), v_ref[rows, cols], preferred_element_type=jnp.float32
            )
        return carry

    lax.fori_loop(first_ref[i], last_ref[i], step, 0)
    lane = lax.broadcasted_iota(jnp.int32, (bq, E), 1)
    lse_all = jnp.zeros((bq, E), jnp.float32)
    for h in range(heads):
        total = jnp.maximum(l_ref[h], 1e-30)
        o_ref[:, h * E:(h + 1) * E] = (acc_ref[h] / total).astype(o_ref.dtype)
        lse_all = jnp.where(lane == h, m_ref[h] + jnp.log2(total), lse_all)
    lse_ref[...] = lse_all


def flash(q, k, v, lo, hi, bq=512, bk=512):
    nq, width = q.shape
    nk = k.shape[0]
    heads = width // E
    bq, bk = min(bq, nq), min(bk, nk)
    blocks = nq // bq
    first = jnp.maximum(jnp.min(lo.reshape(blocks, bq), axis=1), 0) // bk
    last = jnp.minimum(jnp.max(hi.reshape(blocks, bq), axis=1), nk - 1) // bk + 1
    whole = pl.BlockSpec((nk, width), lambda i, *_: (0, 0))
    return pl.pallas_call(
        functools.partial(flash_kernel, heads=heads, bk=bk),
        grid_spec=pltpu.PrefetchScalarGridSpec(
            num_scalar_prefetch=2,
            grid=(blocks,),
            in_specs=[
                pl.BlockSpec((bq, 1), lambda i, *_: (i, 0)),
                pl.BlockSpec((bq, 1), lambda i, *_: (i, 0)),
                pl.BlockSpec((bq, width), lambda i, *_: (i, 0)),
                whole,
                whole,
            ],
            out_specs=[
                pl.BlockSpec((bq, width), lambda i, *_: (i, 0)),
                pl.BlockSpec((bq, E), lambda i, *_: (i, 0)),
            ],
            scratch_shapes=[
                pltpu.VMEM((heads, bq, E), jnp.float32),
                pltpu.VMEM((heads, bq, E), jnp.float32),
                pltpu.VMEM((heads, bq, E), jnp.float32),
            ],
        ),
        out_shape=[
            jax.ShapeDtypeStruct((nq, width), jnp.bfloat16),
            jax.ShapeDtypeStruct((nq, E), jnp.float32),
        ],
        compiler_params=pltpu.CompilerParams(vmem_limit_bytes=48 << 20),
        cost_estimate=pl.CostEstimate(
            flops=nq * nk * width, bytes_accessed=4 * (nq + nk) * width,
            transcendentals=nq * nk * heads // 4,
        ),
        name="attend",
    )(first, last, lo[:, None], hi[:, None], q, k, v)


def row_layout(doc_lengths, image_row, image_slot, length, patch_count):
    row_index = lax.axis_index("dp")
    slot_count = length // patch_count
    lengths = doc_lengths[0]
    ends = jnp.cumsum(lengths)
    starts = ends - lengths
    positions = jnp.arange(length, dtype=jnp.int32)
    inside = (positions[:, None] >= starts[None, :]) & (positions[:, None] < ends[None, :])
    doc_start = jnp.sum(jnp.where(inside, starts[None, :], 0), axis=1)
    doc_end = jnp.sum(jnp.where(inside, ends[None, :], 0), axis=1)
    slot_ids = jnp.arange(slot_count, dtype=jnp.int32)
    picks = (image_slot[None, :] == slot_ids[:, None]) & (image_row == row_index)[None, :]
    slot_used = jnp.any(picks, axis=1)
    slot_image = jnp.argmax(picks, axis=1)
    slot_end = (positions // patch_count + 1) * patch_count
    hi = jnp.where(
        jnp.repeat(slot_used, patch_count), jnp.minimum(slot_end, doc_end) - 1, positions
    )
    return doc_start.astype(jnp.int32), hi.astype(jnp.int32), slot_used, slot_image


def body(projections, doc_lengths, latents, mix_weight, head_weight, image_row, image_slot):
    patch_count, patch_width = latents.shape[1:]
    width = head_weight.shape[2]
    length = projections.shape[1] * lax.axis_size("seq")
    lo, hi, slot_used, slot_image = row_layout(
        doc_lengths, image_row, image_slot, length, patch_count
    )
    every = lax.all_gather(latents, "dp", axis=0, tiled=True)
    mine = jnp.where(slot_used[:, None, None], every[slot_image], 0)
    hidden = down_block(mine.reshape(length, patch_width), mix_weight)
    parts = []
    for part in range(3):
        received = lax.all_to_all(
            projections[0, :, part], "seq", split_axis=1, concat_axis=0, tiled=True
        )
        term = jnp.dot(
            hidden, head_weight[:, part], preferred_element_type=jnp.float32
        ).astype(jnp.bfloat16)
        parts.append(
            (received.astype(jnp.float32) + term.astype(jnp.float32)).astype(jnp.bfloat16)
        )
    result, _ = flash(*parts, lo, hi)
    return lax.all_to_all(result, "seq", split_axis=0, concat_axis=1, tiled=True)[None]


def solution(mesh):
    return jax.shard_map(
        body,
        mesh=mesh,
        in_specs=(
            P("dp", "seq", None, None),
            P("dp", None),
            P("dp", None, None),
            P(),
            P(None, None, "seq"),
            P(),
            P(),
        ),
        out_specs=P("dp", "seq", None),
        check_vma=False,
    )
```

```python
import functools
import math

import jax
import jax.numpy as jnp
from jax import lax
from jax.experimental import pallas as pl
from jax.experimental.pallas import tpu as pltpu
from jax.sharding import PartitionSpec as P

EPSILON = 1e-05
MAX_DOC = 2048
FAR = 1 << 24
SENT_KEYS = 4
GROUP = 4
E = 128
MASKED = -1e30
LOWEST = -1e29
LOG2E = 1.4426950408889634

def flash_kernel(first_ref, last_ref, lo_ref, hi_ref, q_ref, k_ref, v_ref, o_ref, lse_ref,
                 m_ref, l_ref, acc_ref, bias_ref, *, heads, bk):
    i = pl.program_id(0)
    bq = q_ref.shape[0]
    lo = lo_ref[...]
    hi = hi_ref[...]
    scale = LOG2E / math.sqrt(E)
    m_ref[...] = jnp.full(m_ref.shape, LOWEST, jnp.float32)
    l_ref[...] = jnp.zeros(l_ref.shape, jnp.float32)
    acc_ref[...] = jnp.zeros(acc_ref.shape, jnp.float32)

    def step(j, carry):
        rows = pl.ds(pl.multiple_of(j * bk, bk), bk)
        u = j * bk + lax.broadcasted_iota(jnp.int32, (bk, bq), 0)
        bias_ref[...] = jnp.where((u >= lo) & (u <= hi), 0.0, MASKED)
        for h in range(heads):
            cols = slice(h * E, (h + 1) * E)
            s = lax.dot_general(
                k_ref[rows, cols], q_ref[:, cols], (((1,), (1,)), ((), ())),
                preferred_element_type=jnp.float32,
            ) * scale + bias_ref[...]
            m_old = m_ref[h:h + 1]
            m_new = jnp.maximum(m_old, jnp.max(s, axis=0, keepdims=True))
            p = jnp.exp2(s - m_new)
            alpha = jnp.exp2(m_old - m_new)
            m_ref[h:h + 1] = m_new
            l_ref[h:h + 1] = l_ref[h:h + 1] * alpha + jnp.sum(p, axis=0, keepdims=True)
            acc_ref[h] = acc_ref[h] * alpha + lax.dot_general(
                v_ref[rows, cols], p.astype(jnp.bfloat16), (((0,), (0,)), ((), ())),
                preferred_element_type=jnp.float32,
            )
        return carry

    lax.fori_loop(first_ref[i], last_ref[i], step, 0)
    total = jnp.maximum(l_ref[...], 1e-30)
    lse_ref[...] = m_ref[...] + jnp.log2(total)
    for h in range(heads):
        o_ref[:, h * E:(h + 1) * E] = (acc_ref[h] / total[h:h + 1]).T.astype(o_ref.dtype)


def flash(q, k, v, lo, hi, bq=512, bk=512):
    nq, width = q.shape
    nk = k.shape[0]
    heads = width // E
    bq, bk = math.gcd(bq, nq), math.gcd(bk, nk)
    blocks = nq // bq
    first = jnp.maximum(jnp.min(lo.reshape(blocks, bq), axis=1), 0) // bk
    last = jnp.minimum(jnp.max(hi.reshape(blocks, bq), axis=1), nk - 1) // bk + 1
    whole = pl.BlockSpec((nk, width), lambda i, *_: (0, 0))
    return pl.pallas_call(
        functools.partial(flash_kernel, heads=heads, bk=bk),
        grid_spec=pltpu.PrefetchScalarGridSpec(
            num_scalar_prefetch=2,
            grid=(blocks,),
            in_specs=[
                pl.BlockSpec((1, bq), lambda i, *_: (0, i)),
                pl.BlockSpec((1, bq), lambda i, *_: (0, i)),
                pl.BlockSpec((bq, width), lambda i, *_: (i, 0)),
                whole,
                whole,
            ],
            out_specs=[
                pl.BlockSpec((bq, width), lambda i, *_: (i, 0)),
                pl.BlockSpec((heads, bq), lambda i, *_: (0, i)),
            ],
            scratch_shapes=[
                pltpu.VMEM((heads, bq), jnp.float32),
                pltpu.VMEM((heads, bq), jnp.float32),
                pltpu.VMEM((heads, E, bq), jnp.float32),
                pltpu.VMEM((bk, bq), jnp.float32),
            ],
        ),
        out_shape=[
            jax.ShapeDtypeStruct((nq, width), jnp.bfloat16),
            jax.ShapeDtypeStruct((heads, nq), jnp.float32),
        ],
        compiler_params=pltpu.CompilerParams(vmem_limit_bytes=48 << 20),
        cost_estimate=pl.CostEstimate(
            flops=nq * nk * width, bytes_accessed=4 * (nq + nk) * width,
            transcendentals=nq * nk * heads // 4,
        ),
        name="attend",
    )(first, last, lo[None], hi[None], q, k, v)


def merge_kernel(o1_ref, l1_ref, o2_ref, l2_ref, o_ref, lse_ref):
    heads, bq = l1_ref.shape
    first, second = l1_ref[...], l2_ref[...]
    top = jnp.maximum(first, second)
    w1 = jnp.exp2(first - top)
    w2 = jnp.exp2(second - top)
    total = w1 + w2
    lse_ref[...] = top + jnp.log2(total)
    w1 = w1 / total
    w2 = w2 / total
    for h in range(heads):
        cols = slice(h * E, (h + 1) * E)
        a = jnp.broadcast_to(w1[h:h + 1], (E, bq)).T
        b = jnp.broadcast_to(w2[h:h + 1], (E, bq)).T
        o_ref[:, cols] = (
            o1_ref[:, cols].astype(jnp.float32) * a + o2_ref[:, cols].astype(jnp.float32) * b
        ).astype(o_ref.dtype)


def merge(one, two, bq=512):
    rows, width = one[0].shape
    heads = width // E
    bq = min(bq, rows)
    wide = pl.BlockSpec((bq, width), lambda i: (i, 0))
    flat = pl.BlockSpec((heads, bq), lambda i: (0, i))
    return pl.pallas_call(
        merge_kernel,
        grid=(rows // bq,),
        in_specs=[wide, flat, wide, flat],
        out_specs=[wide, flat],
        out_shape=[
            jax.ShapeDtypeStruct((rows, width), jnp.bfloat16),
            jax.ShapeDtypeStruct((heads, rows), jnp.float32),
        ],
        cost_estimate=pl.CostEstimate(
            flops=4 * rows * width, bytes_accessed=6 * rows * width, transcendentals=0
        ),
        name="merge",
    )(*one, *two)


def down_block(patches, mix_weight):
    mixed_rows = jnp.dot(patches, mix_weight, preferred_element_type=jnp.float32)
    scaled = mixed_rows * lax.rsqrt(
        jnp.mean(mixed_rows * mixed_rows, axis=-1, keepdims=True) + EPSILON
    )
    return jax.nn.silu(scaled).astype(jnp.bfloat16)


def row_layout(doc_lengths, slot_used, length, patch_count):
    lengths = doc_lengths[0]
    ends = jnp.cumsum(lengths)
    starts = ends - lengths
    positions = jnp.arange(length, dtype=jnp.int32)
    inside = (positions[None, :] >= starts[:, None]) & (positions[None, :] < ends[:, None])
    doc_start = jnp.sum(jnp.where(inside, starts[:, None], 0), axis=0)
    doc_end = jnp.sum(jnp.where(inside, ends[:, None], 0), axis=0)
    slot_end = (positions // patch_count + 1) * patch_count
    hi = jnp.where(
        jnp.repeat(slot_used, patch_count), jnp.minimum(slot_end, doc_end) - 1, positions
    )
    return doc_start.astype(jnp.int32), hi.astype(jnp.int32)


def row_images(latents, image_row, image_slot, slot_count):
    owners = lax.axis_size("dp")
    row_index = lax.axis_index("dp")
    per_owner = latents.shape[0]
    capacity = (per_owner + per_owner * (owners - 1) // owners + owners - 1) // owners
    table = image_row.reshape(owners, per_owner)
    ids = jnp.arange(per_owner, dtype=jnp.int32)
    same = (table[:, :, None] == table[:, None, :]) & (ids[None, :] < ids[:, None])[None]
    rank = jnp.sum(same.astype(jnp.int32), axis=2)
    my_rows = lax.dynamic_index_in_dim(table, row_index, 0, keepdims=False)
    my_ranks = lax.dynamic_index_in_dim(rank, row_index, 0, keepdims=False)
    place = my_rows * capacity + my_ranks
    chosen = jnp.argmax(
        place[None, :] == jnp.arange(owners * capacity, dtype=jnp.int32)[:, None], axis=1
    )
    received = lax.all_to_all(latents[chosen], "dp", split_axis=0, concat_axis=0, tiled=True)
    slot_ids = jnp.arange(slot_count, dtype=jnp.int32)
    picks = (image_slot[None, :] == slot_ids[:, None]) & (image_row == row_index)[None, :]
    image = jnp.argmax(picks, axis=1).astype(jnp.int32)
    source = image // per_owner * capacity + rank.reshape(-1)[image]
    return received, source, jnp.any(picks, axis=1)


def gather_weights(head_weight):
    owners = lax.axis_size("dp")
    depth, parts, width = head_weight.shape
    share = depth // owners
    mine = lax.dynamic_slice_in_dim(head_weight, lax.axis_index("dp") * share, share, 0)
    columns = lax.all_gather(jnp.transpose(mine, (1, 0, 2)), "seq", axis=0)
    whole = lax.all_gather(columns, "dp", axis=0)
    return [
        jnp.transpose(whole[:, :, part], (0, 2, 1, 3)).reshape(depth, -1) for part in range(parts)
    ]


def add_term(base, hidden, weight):
    term = jnp.dot(hidden, weight, preferred_element_type=jnp.float32).astype(jnp.bfloat16)
    return (base.astype(jnp.float32) + term.astype(jnp.float32)).astype(jnp.bfloat16)


def body(projections, doc_lengths, latents, mix_weight, head_weight, image_row, image_slot):
    patch_count, patch_width = latents.shape[1:]
    shards = lax.axis_size("seq")
    me = lax.axis_index("seq")
    local = projections.shape[1]
    length = local * shards
    slots = local // patch_count
    hops = min(shards - 1, -(-(MAX_DOC - 1) // local))
    down = [(s, s - 1) for s in range(1, shards)]
    up = [(s, s + 1) for s in range(shards - 1)]
    total_heads = projections.shape[3] // E

    def columns(first, count):
        return slice(first * E, (first + count) * E)

    groups = [
        columns(first, min(GROUP, total_heads - first))
        for first in range(SENT_KEYS, total_heads, GROUP)
    ]
    near = columns(0, SENT_KEYS)

    received, source, slot_used = row_images(latents, image_row, image_slot, shards * slots)
    weights = gather_weights(head_weight)
    lo, hi = row_layout(doc_lengths, slot_used, length, patch_count)

    keys = [projections[0, :, 1, near]]
    values = [projections[0, :, 2, near]]
    for _ in range(hops):
        keys.append(lax.ppermute(keys[-1], "seq", up))
        values.append(lax.ppermute(values[-1], "seq", up))
    queries = []
    for group in groups:
        chain = [projections[0, :, 0, group]]
        for _ in range(hops):
            chain.append(lax.ppermute(chain[-1], "seq", down))
        queries.append(chain)

    window = (me - hops) * slots + jnp.arange((2 * hops + 1) * slots, dtype=jnp.int32)
    valid = (window >= 0) & (window < shards * slots)
    clipped = jnp.clip(window, 0, shards * slots - 1)
    used = valid & slot_used[clipped]
    patches = jnp.where(used[:, None, None], received[source[clipped]], 0)
    hidden = down_block(patches.reshape(-1, patch_width), mix_weight)

    def hidden_of(first, count=1):
        return hidden[(hops + first) * local:(hops + first + count) * local]

    far = jnp.full((hops * local,), FAR, jnp.int32)
    lo_after = lax.dynamic_slice_in_dim(jnp.concatenate([lo, far]), me * local, (hops + 1) * local)
    hi_after = lax.dynamic_slice_in_dim(
        jnp.concatenate([hi, -far]), me * local, (hops + 1) * local
    )

    partials = []
    for group, chain in zip(groups, queries):
        key = add_term(projections[0, :, 1, group], hidden_of(0), weights[1][:, group])
        value = add_term(projections[0, :, 2, group], hidden_of(0), weights[2][:, group])
        row = [None] * (hops + 1)
        for r in range(hops, -1, -1):
            query = add_term(chain[r], hidden_of(r), weights[0][:, group])
            rows = slice(r * local, (r + 1) * local)
            row[r] = flash(
                query, key, value, lo_after[rows] - me * local, hi_after[rows] - me * local
            )
        partials.append(row)
    outs = []
    base = (me - hops) * local
    key = add_term(jnp.concatenate(keys[::-1]), hidden_of(-hops, hops + 1), weights[1][:, near])
    value = add_term(jnp.concatenate(values[::-1]), hidden_of(-hops, hops + 1), weights[2][:, near])
    query = add_term(projections[0, :, 0, near], hidden_of(0), weights[0][:, near])
    outs.append(flash(query, key, value, lo_after[:local] - base, hi_after[:local] - base)[0])
    for row in partials:
        carry = row[hops]
        for r in range(hops - 1, -1, -1):
            out = lax.ppermute(carry[0], "seq", up)
            lse = jnp.where(me == 0, LOWEST, lax.ppermute(carry[1], "seq", up))
            carry = merge((out, lse), row[r])
        outs.append(carry[0])
    return jnp.concatenate(outs, axis=1)[None]


def solution(mesh):
    return jax.shard_map(
        body,
        mesh=mesh,
        in_specs=(
            P("dp", "seq", None, None),
            P("dp", None),
            P("dp", None, None),
            P(),
            P(None, None, "seq"),
            P(),
            P(),
        ),
        out_specs=P("dp", "seq", None),
        check_vma=False,
    )
```

```python
import functools
import math

import jax
import jax.numpy as jnp
from jax import lax
from jax.experimental import pallas as pl
from jax.experimental.pallas import tpu as pltpu
from jax.sharding import PartitionSpec as P

EPSILON = 1e-05
MAX_DOC = 2048
FAR = 1 << 24
SENT_KEYS = 4
GROUP = 4
E = 128
MASKED = -1e30
LOWEST = -1e29
LOG2E = 1.4426950408889634

def flash_kernel(first_ref, last_ref, lo_ref, hi_ref, q_ref, k_ref, v_ref, *rest, heads, bk):
    o_ref, lse_ref, m_ref, l_ref, acc_ref, bias_ref = rest[-6:]
    i = pl.program_id(0)
    bq = q_ref.shape[0]
    lo = lo_ref[...]
    hi = hi_ref[...]
    scale = LOG2E / math.sqrt(E)
    m_ref[...] = jnp.full(m_ref.shape, LOWEST, jnp.float32)
    l_ref[...] = jnp.zeros(l_ref.shape, jnp.float32)
    acc_ref[...] = jnp.zeros(acc_ref.shape, jnp.float32)

    def step(j, carry):
        rows = pl.ds(pl.multiple_of(j * bk, bk), bk)
        u = j * bk + lax.broadcasted_iota(jnp.int32, (bk, bq), 0)
        bias_ref[...] = jnp.where((u >= lo) & (u <= hi), 0.0, MASKED)
        for h in range(heads):
            cols = slice(h * E, (h + 1) * E)
            s = lax.dot_general(
                k_ref[rows, cols], q_ref[:, cols], (((1,), (1,)), ((), ())),
                preferred_element_type=jnp.float32,
            ) * scale + bias_ref[...]
            m_old = m_ref[h:h + 1]
            m_new = jnp.maximum(m_old, jnp.max(s, axis=0, keepdims=True))
            p = jnp.exp2(s - m_new)
            alpha = jnp.exp2(m_old - m_new)
            m_ref[h:h + 1] = m_new
            l_ref[h:h + 1] = l_ref[h:h + 1] * alpha + jnp.sum(p, axis=0, keepdims=True)
            acc_ref[h] = acc_ref[h] * alpha + lax.dot_general(
                v_ref[rows, cols], p.astype(jnp.bfloat16), (((0,), (0,)), ((), ())),
                preferred_element_type=jnp.float32,
            )
        return carry

    lax.fori_loop(first_ref[i], last_ref[i], step, 0)
    total = jnp.maximum(l_ref[...], 1e-30)
    lse_ref[...] = m_ref[...] + jnp.log2(total)
    for h in range(heads):
        o_ref[:, h * E:(h + 1) * E] = (acc_ref[h] / total[h:h + 1]).T.astype(o_ref.dtype)


def flash(q, k, v, lo, hi, earlier=(), bq=512, bk=512):
    nq, width = q.shape
    nk = k.shape[0]
    heads = width // E
    bq, bk = math.gcd(bq, nq), math.gcd(bk, nk)
    blocks = nq // bq
    first = jnp.maximum(jnp.min(lo.reshape(blocks, bq), axis=1), 0) // bk
    last = jnp.minimum(jnp.max(hi.reshape(blocks, bq), axis=1), nk - 1) // bk + 1
    whole = pl.BlockSpec((nk, width), lambda i, *_: (0, 0))
    return pl.pallas_call(
        functools.partial(flash_kernel, heads=heads, bk=bk),
        grid_spec=pltpu.PrefetchScalarGridSpec(
            num_scalar_prefetch=2,
            grid=(blocks,),
            in_specs=[
                pl.BlockSpec((1, bq), lambda i, *_: (0, i)),
                pl.BlockSpec((1, bq), lambda i, *_: (0, i)),
                pl.BlockSpec((bq, width), lambda i, *_: (i, 0)),
                whole,
                whole,
            ] + [pl.BlockSpec(memory_space=pl.ANY)] * len(earlier),
            out_specs=[
                pl.BlockSpec((bq, width), lambda i, *_: (i, 0)),
                pl.BlockSpec((heads, bq), lambda i, *_: (0, i)),
            ],
            scratch_shapes=[
                pltpu.VMEM((heads, bq), jnp.float32),
                pltpu.VMEM((heads, bq), jnp.float32),
                pltpu.VMEM((heads, E, bq), jnp.float32),
                pltpu.VMEM((bk, bq), jnp.float32),
            ],
        ),
        out_shape=[
            jax.ShapeDtypeStruct((nq, width), jnp.bfloat16),
            jax.ShapeDtypeStruct((heads, nq), jnp.float32),
        ],
        compiler_params=pltpu.CompilerParams(vmem_limit_bytes=48 << 20),
        cost_estimate=pl.CostEstimate(
            flops=nq * nk * width, bytes_accessed=4 * (nq + nk) * width,
            transcendentals=nq * nk * heads // 4,
        ),
        name="attend",
    )(first, last, lo[None], hi[None], q, k, v, *earlier)


def merge_kernel(o1_ref, l1_ref, o2_ref, l2_ref, *rest):
    o_ref, lse_ref = rest[-2:]
    heads, bq = l1_ref.shape
    first, second = l1_ref[...], l2_ref[...]
    top = jnp.maximum(first, second)
    w1 = jnp.exp2(first - top)
    w2 = jnp.exp2(second - top)
    total = w1 + w2
    lse_ref[...] = top + jnp.log2(total)
    w1 = w1 / total
    w2 = w2 / total
    for h in range(heads):
        cols = slice(h * E, (h + 1) * E)
        a = jnp.broadcast_to(w1[h:h + 1], (E, bq)).T
        b = jnp.broadcast_to(w2[h:h + 1], (E, bq)).T
        o_ref[:, cols] = (
            o1_ref[:, cols].astype(jnp.float32) * a + o2_ref[:, cols].astype(jnp.float32) * b
        ).astype(o_ref.dtype)


def merge(one, two, earlier=(), bq=512):
    rows, width = one[0].shape
    heads = width // E
    bq = min(bq, rows)
    wide = pl.BlockSpec((bq, width), lambda i: (i, 0))
    flat = pl.BlockSpec((heads, bq), lambda i: (0, i))
    return pl.pallas_call(
        merge_kernel,
        grid=(rows // bq,),
        in_specs=[wide, flat, wide, flat] + [pl.BlockSpec(memory_space=pl.ANY)] * len(earlier),
        out_specs=[wide, flat],
        out_shape=[
            jax.ShapeDtypeStruct((rows, width), jnp.bfloat16),
            jax.ShapeDtypeStruct((heads, rows), jnp.float32),
        ],
        cost_estimate=pl.CostEstimate(
            flops=4 * rows * width, bytes_accessed=6 * rows * width, transcendentals=0
        ),
        name="merge",
    )(*one, *two, *earlier)


def down_block(patches, mix_weight):
    mixed_rows = jnp.dot(patches, mix_weight, preferred_element_type=jnp.float32)
    scaled = mixed_rows * lax.rsqrt(
        jnp.mean(mixed_rows * mixed_rows, axis=-1, keepdims=True) + EPSILON
    )
    return jax.nn.silu(scaled).astype(jnp.bfloat16)


def row_layout(doc_lengths, slot_used, length, patch_count):
    lengths = doc_lengths[0]
    ends = jnp.cumsum(lengths)
    starts = ends - lengths
    positions = jnp.arange(length, dtype=jnp.int32)
    inside = (positions[None, :] >= starts[:, None]) & (positions[None, :] < ends[:, None])
    doc_start = jnp.sum(jnp.where(inside, starts[:, None], 0), axis=0)
    doc_end = jnp.sum(jnp.where(inside, ends[:, None], 0), axis=0)
    slot_end = (positions // patch_count + 1) * patch_count
    hi = jnp.where(
        jnp.repeat(slot_used, patch_count), jnp.minimum(slot_end, doc_end) - 1, positions
    )
    return doc_start.astype(jnp.int32), hi.astype(jnp.int32)


def row_images(latents, image_row, image_slot, slot_count):
    owners = lax.axis_size("dp")
    row_index = lax.axis_index("dp")
    per_owner = latents.shape[0]
    capacity = (per_owner + per_owner * (owners - 1) // owners + owners - 1) // owners
    table = image_row.reshape(owners, per_owner)
    ids = jnp.arange(per_owner, dtype=jnp.int32)
    same = (table[:, :, None] == table[:, None, :]) & (ids[None, :] < ids[:, None])[None]
    rank = jnp.sum(same.astype(jnp.int32), axis=2)
    my_rows = lax.dynamic_index_in_dim(table, row_index, 0, keepdims=False)
    my_ranks = lax.dynamic_index_in_dim(rank, row_index, 0, keepdims=False)
    place = my_rows * capacity + my_ranks
    chosen = jnp.argmax(
        place[None, :] == jnp.arange(owners * capacity, dtype=jnp.int32)[:, None], axis=1
    )
    received = lax.all_to_all(latents[chosen], "dp", split_axis=0, concat_axis=0, tiled=True)
    slot_ids = jnp.arange(slot_count, dtype=jnp.int32)
    picks = (image_slot[None, :] == slot_ids[:, None]) & (image_row == row_index)[None, :]
    image = jnp.argmax(picks, axis=1).astype(jnp.int32)
    source = image // per_owner * capacity + rank.reshape(-1)[image]
    return received, source, jnp.any(picks, axis=1)


def weight_pieces(head_weight):
    shards = lax.axis_size("seq")
    me = lax.axis_index("seq")
    share = head_weight.shape[0] // lax.axis_size("dp")
    mine = lax.dynamic_slice_in_dim(head_weight, lax.axis_index("dp") * share, share, 0)
    mine = jnp.transpose(mine, (1, 0, 2))
    turned = [mine]
    for k in range(1, shards):
        pairs = [(s, (s + k) % shards) for s in range(shards)]
        turned.append(lax.ppermute(mine, "seq", pairs))
    turned = jnp.stack(turned)
    return [
        lax.dynamic_index_in_dim(turned, (me - z + shards) % shards, 0, keepdims=False)
        for z in range(shards)
    ]


def gather_columns(pieces, columns):
    width = pieces[0].shape[2]
    first, last = columns.start // width, -(-columns.stop // width)
    near = jnp.concatenate(pieces[first:last], axis=2)
    near = near[:, :, columns.start - first * width:columns.stop - first * width]
    return lax.all_gather(near, "dp", axis=0)


def add_term_kernel(base_ref, hidden_ref, weight_ref, *rest):
    weight = weight_ref[...].reshape(hidden_ref.shape[1], -1)
    term = jnp.dot(hidden_ref[...], weight, preferred_element_type=jnp.float32)
    term = term.astype(jnp.bfloat16).astype(jnp.float32)
    rest[-1][...] = (base_ref[...].astype(jnp.float32) + term).astype(jnp.bfloat16)


def add_term(base, base_part, base_column, hidden, hidden_row, rows, weight, part, earlier):
    shares, _, share, width = weight.shape
    depth = hidden.shape[1]
    bq = math.gcd(512, rows)
    base_column, hidden_row = base_column // width, hidden_row // bq
    return pl.pallas_call(
        add_term_kernel,
        grid=(rows // bq,),
        in_specs=[
            pl.BlockSpec((None, bq, width), lambda i: (base_part, i, base_column)),
            pl.BlockSpec((bq, depth), lambda i: (hidden_row + i, 0)),
            pl.BlockSpec((shares, None, share, width), lambda i: (0, part, 0, 0)),
        ] + [pl.BlockSpec(memory_space=pl.ANY)] * len(earlier),
        out_specs=pl.BlockSpec((bq, width), lambda i: (i, 0)),
        out_shape=jax.ShapeDtypeStruct((rows, width), jnp.bfloat16),
        compiler_params=pltpu.CompilerParams(vmem_limit_bytes=32 << 20),
        cost_estimate=pl.CostEstimate(
            flops=2 * rows * width * depth, bytes_accessed=8 * rows * width, transcendentals=0
        ),
        name="add_term",
    )(base, hidden, weight, *earlier)


def body(projections, doc_lengths, latents, mix_weight, head_weight, image_row, image_slot):
    patch_count, patch_width = latents.shape[1:]
    shards = lax.axis_size("seq")
    me = lax.axis_index("seq")
    local = projections.shape[1]
    length = local * shards
    slots = local // patch_count
    hops = min(shards - 1, -(-(MAX_DOC - 1) // local))
    down = [(s, s - 1) for s in range(1, shards)]
    up = [(s, s + 1) for s in range(shards - 1)]
    total_heads = projections.shape[3] // E

    def columns(first, count):
        return slice(first * E, (first + count) * E)

    groups = [
        columns(first, min(GROUP, total_heads - first))
        for first in range(SENT_KEYS, total_heads, GROUP)
    ]
    near = columns(0, SENT_KEYS)

    received, source, slot_used = row_images(latents, image_row, image_slot, shards * slots)
    pieces = weight_pieces(head_weight)
    weights = [gather_columns(pieces, group) for group in groups]
    near_weights = gather_columns(pieces, near)
    lo, hi = row_layout(doc_lengths, slot_used, length, patch_count)

    keys = [projections[0, :, 1, near]]
    values = [projections[0, :, 2, near]]
    for _ in range(hops):
        keys.append(lax.ppermute(keys[-1], "seq", up))
        values.append(lax.ppermute(values[-1], "seq", up))
    queries = []
    for group in groups:
        first = projections[0, :, 0, group]
        if queries and hops:
            first = lax.optimization_barrier((first, queries[-1][1]))[0]
        chain = [first]
        for _ in range(hops):
            chain.append(lax.ppermute(chain[-1], "seq", down))
        queries.append(chain)

    window = (me - hops) * slots + jnp.arange((2 * hops + 1) * slots, dtype=jnp.int32)
    valid = (window >= 0) & (window < shards * slots)
    clipped = jnp.clip(window, 0, shards * slots - 1)
    used = valid & slot_used[clipped]
    patches = jnp.where(used[:, None, None], received[source[clipped]], 0)
    hidden = down_block(patches.reshape(-1, patch_width), mix_weight)

    own = jnp.transpose(projections[0], (1, 0, 2))
    far = jnp.full((hops * local,), FAR, jnp.int32)
    lo_after = lax.dynamic_slice_in_dim(jnp.concatenate([lo, far]), me * local, (hops + 1) * local)
    hi_after = lax.dynamic_slice_in_dim(
        jnp.concatenate([hi, -far]), me * local, (hops + 1) * local
    )

    carry = [None] * len(groups)
    partial = {}
    combined = {}
    last = ()

    def attend(g, r, last):
        start = groups[g].start
        if g not in combined:
            combined[g] = [
                add_term(own, part, start, hidden, hops * local, local, weights[g], part, last)
                for part in (1, 2)
            ]
        base, column = (queries[g][r][None], 0) if r else (own, start)
        query = add_term(
            base, 0, column, hidden, (hops + r) * local, local, weights[g], 0, last
        )
        rows = slice(r * local, (r + 1) * local)
        partial[g, r] = flash(
            query, *combined[g], lo_after[rows] - me * local, hi_after[rows] - me * local, last
        )
        return (partial[g, r][1],)

    def pass_on(g):
        out = lax.ppermute(carry[g][0], "seq", up)
        lse = jnp.where(me == 0, LOWEST, lax.ppermute(carry[g][1], "seq", up))
        return out, lse

    steps = [(g + 2 * (hops - r), r, g) for g in range(len(groups)) for r in range(1, hops + 1)]
    for _, r, g in sorted(steps):
        last = attend(g, r, last)
        if r < hops:
            carry[g] = merge(carry[g], partial[g, r], last)
            last = (carry[g][1],)
        else:
            carry[g] = partial[g, r]
        carry[g] = pass_on(g)
    base = (me - hops) * local
    key, value = [
        add_term(
            jnp.concatenate(chain[::-1])[None], 0, 0, hidden, 0, (hops + 1) * local,
            near_weights, part, last,
        )
        for part, chain in ((1, keys), (2, values))
    ]
    query = add_term(own, 0, 0, hidden, hops * local, local, near_weights, 0, last)
    result = flash(query, key, value, lo_after[:local] - base, hi_after[:local] - base, last)
    outs = [result[0]]
    last = (result[1],)
    for g in range(len(groups)):
        last = attend(g, 0, last)
    for g in range(len(groups)):
        done = merge(carry[g], partial[g, 0], last)
        last = (done[1],)
        outs.append(done[0])
    return jnp.concatenate(outs, axis=1)[None]


def solution(mesh):
    return jax.shard_map(
        body,
        mesh=mesh,
        in_specs=(
            P("dp", "seq", None, None),
            P("dp", None),
            P("dp", None, None),
            P(),
            P(None, None, "seq"),
            P(),
            P(),
        ),
        out_specs=P("dp", "seq", None),
        check_vma=False,
    )
```

```python
import functools
import math

import jax
import jax.numpy as jnp
from jax import lax
from jax.experimental import pallas as pl
from jax.experimental.pallas import tpu as pltpu
from jax.sharding import PartitionSpec as P

EPSILON = 1e-05
MAX_DOC = 2048
FAR = 1 << 24
SENT_KEYS = 4
GROUP = 4
E = 128
MASKED = -1e30
LOWEST = -1e29
LOG2E = 1.4426950408889634

def flash_kernel(first_ref, last_ref, lo_ref, hi_ref, q_ref, k_ref, v_ref, *rest, heads, bk):
    o_ref, lse_ref, m_ref, l_ref, acc_ref, bias_ref = rest[-6:]
    i = pl.program_id(0)
    bq = q_ref.shape[0]
    lo = lo_ref[...]
    hi = hi_ref[...]
    scale = LOG2E / math.sqrt(E)
    m_ref[...] = jnp.full(m_ref.shape, LOWEST, jnp.float32)
    l_ref[...] = jnp.zeros(l_ref.shape, jnp.float32)
    acc_ref[...] = jnp.zeros(acc_ref.shape, jnp.float32)

    def step(j, carry):
        rows = pl.ds(pl.multiple_of(j * bk, bk), bk)
        u = j * bk + lax.broadcasted_iota(jnp.int32, (bk, bq), 0)
        bias_ref[...] = jnp.where((u >= lo) & (u <= hi), 0.0, MASKED)
        for h in range(heads):
            cols = slice(h * E, (h + 1) * E)
            s = lax.dot_general(
                k_ref[rows, cols], q_ref[:, cols], (((1,), (1,)), ((), ())),
                preferred_element_type=jnp.float32,
            ) * scale + bias_ref[...]
            m_old = m_ref[h:h + 1]
            m_new = jnp.maximum(m_old, jnp.max(s, axis=0, keepdims=True))
            p = jnp.exp2(s - m_new)
            alpha = jnp.exp2(m_old - m_new)
            m_ref[h:h + 1] = m_new
            l_ref[h:h + 1] = l_ref[h:h + 1] * alpha + jnp.sum(p, axis=0, keepdims=True)
            acc_ref[h] = acc_ref[h] * alpha + lax.dot_general(
                v_ref[rows, cols], p.astype(jnp.bfloat16), (((0,), (0,)), ((), ())),
                preferred_element_type=jnp.float32,
            )
        return carry

    lax.fori_loop(first_ref[i], last_ref[i], step, 0)
    total = jnp.maximum(l_ref[...], 1e-30)
    lse_ref[...] = m_ref[...] + jnp.log2(total)
    for h in range(heads):
        o_ref[:, h * E:(h + 1) * E] = (acc_ref[h] / total[h:h + 1]).T.astype(o_ref.dtype)


def flash(q, k, v, lo, hi, earlier=(), bq=512, bk=512):
    nq, width = q.shape
    nk = k.shape[0]
    heads = width // E
    bq, bk = math.gcd(bq, nq), math.gcd(bk, nk)
    blocks = nq // bq
    first = jnp.maximum(jnp.min(lo.reshape(blocks, bq), axis=1), 0) // bk
    last = jnp.minimum(jnp.max(hi.reshape(blocks, bq), axis=1), nk - 1) // bk + 1
    whole = pl.BlockSpec((nk, width), lambda i, *_: (0, 0))
    return pl.pallas_call(
        functools.partial(flash_kernel, heads=heads, bk=bk),
        grid_spec=pltpu.PrefetchScalarGridSpec(
            num_scalar_prefetch=2,
            grid=(blocks,),
            in_specs=[
                pl.BlockSpec((1, bq), lambda i, *_: (0, i)),
                pl.BlockSpec((1, bq), lambda i, *_: (0, i)),
                pl.BlockSpec((bq, width), lambda i, *_: (i, 0)),
                whole,
                whole,
            ] + [pl.BlockSpec(memory_space=pl.ANY)] * len(earlier),
            out_specs=[
                pl.BlockSpec((bq, width), lambda i, *_: (i, 0)),
                pl.BlockSpec((heads, bq), lambda i, *_: (0, i)),
            ],
            scratch_shapes=[
                pltpu.VMEM((heads, bq), jnp.float32),
                pltpu.VMEM((heads, bq), jnp.float32),
                pltpu.VMEM((heads, E, bq), jnp.float32),
                pltpu.VMEM((bk, bq), jnp.float32),
            ],
        ),
        out_shape=[
            jax.ShapeDtypeStruct((nq, width), jnp.bfloat16),
            jax.ShapeDtypeStruct((heads, nq), jnp.float32),
        ],
        compiler_params=pltpu.CompilerParams(vmem_limit_bytes=48 << 20),
        cost_estimate=pl.CostEstimate(
            flops=nq * nk * width, bytes_accessed=4 * (nq + nk) * width,
            transcendentals=nq * nk * heads // 4,
        ),
        name="attend",
    )(first, last, lo[None], hi[None], q, k, v, *earlier)


def merge_kernel(o1_ref, l1_ref, o2_ref, l2_ref, *rest):
    o_ref, lse_ref = rest[-2:]
    heads, bq = l1_ref.shape
    first, second = l1_ref[...], l2_ref[...]
    top = jnp.maximum(first, second)
    w1 = jnp.exp2(first - top)
    w2 = jnp.exp2(second - top)
    total = w1 + w2
    lse_ref[...] = top + jnp.log2(total)
    w1 = w1 / total
    w2 = w2 / total
    for h in range(heads):
        cols = slice(h * E, (h + 1) * E)
        a = jnp.broadcast_to(w1[h:h + 1], (E, bq)).T
        b = jnp.broadcast_to(w2[h:h + 1], (E, bq)).T
        o_ref[:, cols] = (
            o1_ref[:, cols].astype(jnp.float32) * a + o2_ref[:, cols].astype(jnp.float32) * b
        ).astype(o_ref.dtype)


def merge(one, two, earlier=(), bq=512):
    rows, width = one[0].shape
    heads = width // E
    bq = min(bq, rows)
    wide = pl.BlockSpec((bq, width), lambda i: (i, 0))
    flat = pl.BlockSpec((heads, bq), lambda i: (0, i))
    return pl.pallas_call(
        merge_kernel,
        grid=(rows // bq,),
        in_specs=[wide, flat, wide, flat] + [pl.BlockSpec(memory_space=pl.ANY)] * len(earlier),
        out_specs=[wide, flat],
        out_shape=[
            jax.ShapeDtypeStruct((rows, width), jnp.bfloat16),
            jax.ShapeDtypeStruct((heads, rows), jnp.float32),
        ],
        cost_estimate=pl.CostEstimate(
            flops=4 * rows * width, bytes_accessed=6 * rows * width, transcendentals=0
        ),
        name="merge",
    )(*one, *two, *earlier)


def down_block(patches, mix_weight):
    mixed_rows = jnp.dot(patches, mix_weight, preferred_element_type=jnp.float32)
    scaled = mixed_rows * lax.rsqrt(
        jnp.mean(mixed_rows * mixed_rows, axis=-1, keepdims=True) + EPSILON
    )
    return jax.nn.silu(scaled).astype(jnp.bfloat16)


def row_layout(doc_lengths, slot_used, length, patch_count):
    lengths = doc_lengths[0]
    ends = jnp.cumsum(lengths)
    starts = ends - lengths
    positions = jnp.arange(length, dtype=jnp.int32)
    inside = (positions[None, :] >= starts[:, None]) & (positions[None, :] < ends[:, None])
    doc_start = jnp.sum(jnp.where(inside, starts[:, None], 0), axis=0)
    doc_end = jnp.sum(jnp.where(inside, ends[:, None], 0), axis=0)
    slot_end = (positions // patch_count + 1) * patch_count
    hi = jnp.where(
        jnp.repeat(slot_used, patch_count), jnp.minimum(slot_end, doc_end) - 1, positions
    )
    return doc_start.astype(jnp.int32), hi.astype(jnp.int32)


def row_images(latents, image_row, image_slot, slot_count):
    owners = lax.axis_size("dp")
    row_index = lax.axis_index("dp")
    per_owner = latents.shape[0]
    capacity = (per_owner + per_owner * (owners - 1) // owners + owners - 1) // owners
    table = image_row.reshape(owners, per_owner)
    ids = jnp.arange(per_owner, dtype=jnp.int32)
    same = (table[:, :, None] == table[:, None, :]) & (ids[None, :] < ids[:, None])[None]
    rank = jnp.sum(same.astype(jnp.int32), axis=2)
    my_rows = lax.dynamic_index_in_dim(table, row_index, 0, keepdims=False)
    my_ranks = lax.dynamic_index_in_dim(rank, row_index, 0, keepdims=False)
    place = my_rows * capacity + my_ranks
    chosen = jnp.argmax(
        place[None, :] == jnp.arange(owners * capacity, dtype=jnp.int32)[:, None], axis=1
    )
    received = lax.all_to_all(latents[chosen], "dp", split_axis=0, concat_axis=0, tiled=True)
    slot_ids = jnp.arange(slot_count, dtype=jnp.int32)
    picks = (image_slot[None, :] == slot_ids[:, None]) & (image_row == row_index)[None, :]
    image = jnp.argmax(picks, axis=1).astype(jnp.int32)
    source = image // per_owner * capacity + rank.reshape(-1)[image]
    return received, source, jnp.any(picks, axis=1)


def gather_weights(head_weight):
    owners = lax.axis_size("dp")
    depth, parts, width = head_weight.shape
    share = depth // owners
    mine = lax.dynamic_slice_in_dim(head_weight, lax.axis_index("dp") * share, share, 0)
    columns = lax.all_gather(jnp.transpose(mine, (1, 0, 2)), "seq", axis=0)
    whole = lax.all_gather(columns, "dp", axis=0)
    return [
        jnp.transpose(whole[:, :, part], (0, 2, 1, 3)).reshape(depth, -1) for part in range(parts)
    ]


def add_term(base, hidden, weight):
    term = jnp.dot(hidden, weight, preferred_element_type=jnp.float32).astype(jnp.bfloat16)
    return (base.astype(jnp.float32) + term.astype(jnp.float32)).astype(jnp.bfloat16)


def body(projections, doc_lengths, latents, mix_weight, head_weight, image_row, image_slot):
    patch_count, patch_width = latents.shape[1:]
    shards = lax.axis_size("seq")
    me = lax.axis_index("seq")
    local = projections.shape[1]
    length = local * shards
    slots = local // patch_count
    hops = min(shards - 1, -(-(MAX_DOC - 1) // local))
    down = [(s, s - 1) for s in range(1, shards)]
    up = [(s, s + 1) for s in range(shards - 1)]
    total_heads = projections.shape[3] // E

    def columns(first, count):
        return slice(first * E, (first + count) * E)

    groups = [
        columns(first, min(GROUP, total_heads - first))
        for first in range(SENT_KEYS, total_heads, GROUP)
    ]
    near = columns(0, SENT_KEYS)

    received, source, slot_used = row_images(latents, image_row, image_slot, shards * slots)
    whole = gather_weights(head_weight)
    weights = [[part[:, group] for part in whole] for group in groups]
    near_weights = [part[:, near] for part in whole]
    lo, hi = row_layout(doc_lengths, slot_used, length, patch_count)

    keys = [projections[0, :, 1, near]]
    values = [projections[0, :, 2, near]]
    for _ in range(hops):
        keys.append(lax.ppermute(keys[-1], "seq", up))
        values.append(lax.ppermute(values[-1], "seq", up))
    queries = []
    for group in groups:
        chain = [projections[0, :, 0, group]]
        for _ in range(hops):
            chain.append(lax.ppermute(chain[-1], "seq", down))
        queries.append(chain)

    window = (me - hops) * slots + jnp.arange((2 * hops + 1) * slots, dtype=jnp.int32)
    valid = (window >= 0) & (window < shards * slots)
    clipped = jnp.clip(window, 0, shards * slots - 1)
    used = valid & slot_used[clipped]
    patches = jnp.where(used[:, None, None], received[source[clipped]], 0)
    hidden = down_block(patches.reshape(-1, patch_width), mix_weight)

    def hidden_of(first, count=1):
        return hidden[(hops + first) * local:(hops + first + count) * local]

    far = jnp.full((hops * local,), FAR, jnp.int32)
    lo_after = lax.dynamic_slice_in_dim(jnp.concatenate([lo, far]), me * local, (hops + 1) * local)
    hi_after = lax.dynamic_slice_in_dim(
        jnp.concatenate([hi, -far]), me * local, (hops + 1) * local
    )

    combined = []
    for group, weight in zip(groups, weights):
        combined.append([
            add_term(projections[0, :, part, group], hidden_of(0), weight[part])
            for part in (1, 2)
        ])
    carry = [None] * len(groups)
    partial = {}
    last = ()

    def attend(g, r):
        query = add_term(queries[g][r], hidden_of(r), weights[g][0])
        rows = slice(r * local, (r + 1) * local)
        partial[g, r] = flash(
            query, *combined[g], lo_after[rows] - me * local, hi_after[rows] - me * local, last
        )
        return (partial[g, r][1],)

    def pass_on(g):
        out = lax.ppermute(carry[g][0], "seq", up)
        lse = jnp.where(me == 0, LOWEST, lax.ppermute(carry[g][1], "seq", up))
        return out, lse

    steps = [(g + 2 * (hops - r), r, g) for g in range(len(groups)) for r in range(1, hops + 1)]
    for _, r, g in sorted(steps):
        last = attend(g, r)
        if r < hops:
            carry[g] = merge(carry[g], partial[g, r], last)
            last = (carry[g][1],)
        else:
            carry[g] = partial[g, r]
        carry[g] = pass_on(g)
    base = (me - hops) * local
    key = add_term(jnp.concatenate(keys[::-1]), hidden_of(-hops, hops + 1), near_weights[1])
    value = add_term(jnp.concatenate(values[::-1]), hidden_of(-hops, hops + 1), near_weights[2])
    query = add_term(projections[0, :, 0, near], hidden_of(0), near_weights[0])
    result = flash(query, key, value, lo_after[:local] - base, hi_after[:local] - base, last)
    outs = [result[0]]
    last = (result[1],)
    for g in range(len(groups)):
        last = attend(g, 0)
    for g in range(len(groups)):
        done = merge(carry[g], partial[g, 0], last)
        last = (done[1],)
        outs.append(done[0])
    return jnp.concatenate(outs, axis=1)[None]


def solution(mesh):
    return jax.shard_map(
        body,
        mesh=mesh,
        in_specs=(
            P("dp", "seq", None, None),
            P("dp", None),
            P("dp", None, None),
            P(),
            P(None, None, "seq"),
            P(),
            P(),
        ),
        out_specs=P("dp", "seq", None),
        check_vma=False,
    )
```
